32 devices in a mesh: groups: 2 (over y), patch: 4 (over z), head: 4 (over x, core).
Axes of the slice: x: 2, y: 2, z: 4, core: 2. Of those that a mesh axis runs over, the one named last changes fastest.
Arguments:
- qkv: bfloat16 [1024, 3, 3072], P(('groups', 'patch', 'head')), parts along dimension 0, may hold values from -8 to 8
- stale_kv: bfloat16 [1024, 2, 3072], P(('groups', 'patch'), None, 'head'), parts along dimension 0, may hold values from -8 to 8
- w_out: bfloat16 [3072, 3072], P('head'), may hold values from -0.109375 to 0.109375
- gate_table: bfloat16 [50, 3072], replicated, may hold values from -4 to 4
- lengths: int32 [8], P('groups'), parts along dimension 0, may hold values from 1 to 96, 256 in all
- timestep: int32 [2], P('groups'), parts along dimension 0, may hold values from 0 to 49
Outputs:
- branch: bfloat16 [1024, 3072], P(('groups', 'patch', 'head')), parts along dimension 0
- next_kv: bfloat16 [1024, 2, 3072], P(('groups', 'patch'), None, 'head'), parts along dimension 0
The draws below stay inside these ranges and needn't reach their ends.
There are 2 independent parts, one for each index of `groups`. The reference program is written for one: setup_inputs(seed, part) draws one part's arguments, and reference() takes and returns one part's arrays. A program takes and returns all parts, laid end to end along the dimension named above; an argument that names none is the same for every part. Nothing has to cross between parts.
Inputs may be any that keep to these rules, and one draw needn't show every extreme that they name: `lengths`: the live tokens are the first rows of each patch's 128 slots; no patch has more than 96 live tokens, and one has exactly 96.
All inputs are finite; a program needn't handle non-finite values.
Results may differ from the reference program's by a relative error of at most 0.013.
Values may be sent and summed in bfloat16 or wider, within the bound.
No kernel may reach another device: no remote copies, remote signals or barrier semaphores. Data moves between devices by JAX's collectives and lax.ppermute only.
A program may use at most 128 MiB of HBM per device.

```python
import math
import jax
import jax.numpy as jnp
import numpy as np
from jax import lax

D = 3072
HEADS = 24
HEAD_DIM = 128
STEPS = 50
TOK_DEV = 32
TOKENS = 512
MOST_LIVE = 96
LIVE = 256
N_PATCH = 4
N_HEAD = 4


def draw_qkv(key, part):
    key = jax.random.fold_in(key, 11)
    scales = jnp.array([1.6, 1.6, 1.0], jnp.float32)
    drawn = jax.random.normal(key, (TOKENS, 3, D), jnp.float32) * scales[None, :, None]
    drawn = jnp.clip(drawn, -8.0, 8.0)
    return drawn.astype(jnp.bfloat16)


def draw_stale_kv(key, part):
    key = jax.random.fold_in(key, 13)
    scales = jnp.array([1.6, 1.0], jnp.float32)
    drawn = jax.random.normal(key, (TOKENS, 2, D), jnp.float32) * scales[None, :, None]
    drawn = jnp.clip(drawn, -8.0, 8.0)
    return drawn.astype(jnp.bfloat16)


def shard_levels(own_key, dims, split, smallest, largest):
    level = 1.0
    for dim, shards_of in split:
        steps = jax.random.uniform(jax.random.fold_in(jax.random.fold_in(own_key, 6), dim), (shards_of,), jnp.float32, smallest / len(split), largest / len(split))
        level = level * jnp.repeat(jnp.exp(steps), dims[dim] // shards_of).reshape((-1,) + (1,) * (len(dims) - 1 - dim))
    return level


def profile(amount, total, bound, slope):
    portions = [(1 << 20) // math.isqrt(rank ** slope) + 1 for rank in range(2, amount + 1)]
    surplus, given = total - bound - (amount - 1), [1] * (amount - 1)
    while surplus > 0:
        movable = [i for i in range(amount - 1) if given[i] < bound]
        mass, remaining = sum([portions[i] for i in movable]), surplus
        for i in movable:
            addition = min(bound - given[i], max(1, remaining * portions[i] // mass), surplus)
            given[i] = given[i] + addition
            surplus = surplus - addition
    return np.array([bound] + given)


def ragged_sizes(rng, count, total, reach, skew):
    if count == 2:
        one = jax.random.randint(rng, (), max(1, total - reach), min(reach, total - 1) + 1)
        return jnp.stack([one, total - one])
    sizes = jnp.asarray(profile(count, total, reach, skew), jnp.int32)
    couples = (count - 1) // 2
    donor, receiver = sizes[1:1 + 2 * couples:2], sizes[2:2 + 2 * couples:2]
    margin = jnp.minimum(donor - 1, reach - receiver)
    passed = jax.random.randint(jax.random.fold_in(rng, 1), (couples,), 0, 1 << 20) % (margin + 1)
    sizes = sizes.at[1:1 + 2 * couples:2].set(donor - passed).at[2:2 + 2 * couples:2].set(receiver + passed)
    return sizes[jax.random.permutation(jax.random.fold_in(rng, 2), count)]


def bell_draw(rng, extent, spread, limit, cuts=(), kind=jnp.bfloat16):
    result = spread * jax.random.normal(rng, extent, jnp.float32)
    if cuts:
        result = result * shard_levels(rng, extent, cuts, -0.22, 0.18)
    return jnp.clip(result, -limit, limit).astype(kind)


def setup_inputs(seed: int = 0, part: int = 0) -> dict:
    key_list = jax.random.split(jax.random.key(seed), 7)
    own_keys = jax.random.split(jax.random.fold_in(key_list[6], part), 7)
    return {
        "qkv": draw_qkv(jax.random.fold_in(jax.random.fold_in(key_list[6], part), 71), part),
        "stale_kv": draw_stale_kv(jax.random.fold_in(jax.random.fold_in(key_list[6], part), 71), part),
        "w_out": bell_draw(key_list[2], (D, D), D ** -0.5, 0.109375, ((0, 4),)),
        "gate_table": bell_draw(key_list[3], (STEPS, D), 1.0, 4.0),
        "lengths": ragged_sizes(own_keys[4], N_PATCH, LIVE, MOST_LIVE, 1).astype(jnp.int32),
        "timestep": jax.random.randint(own_keys[5], (1,), 0, STEPS).astype(jnp.int32),
    }


def reference(qkv, stale_kv, w_out, gate_table, lengths, timestep):
    patch_rows = TOK_DEV * N_HEAD
    score_scale = 1.0 / math.sqrt(HEAD_DIM)
    positions = jnp.arange(TOKENS, dtype=jnp.int32)
    owners = positions // patch_rows
    within = positions - owners * patch_rows
    usable = within < lengths[owners]

    def one_patch(patch_id):
        first_row = (patch_id * patch_rows).astype(jnp.int32)
        queries = lax.dynamic_slice_in_dim(qkv[:, 0], first_row, patch_rows, 0)
        own_rows = (owners == patch_id)[:, None]
        keys_used = jnp.where(own_rows, qkv[:, 1], stale_kv[:, 0])
        values_used = jnp.where(own_rows, qkv[:, 2], stale_kv[:, 1])
        queries = queries.reshape(patch_rows, HEADS, HEAD_DIM).astype(jnp.float32)
        keys_used = keys_used.reshape(TOKENS, HEADS, HEAD_DIM).astype(jnp.float32)
        values_used = values_used.reshape(TOKENS, HEADS, HEAD_DIM).astype(jnp.float32)
        scores = jnp.einsum('qhe,khe->hqk', queries, keys_used, precision=lax.Precision.HIGHEST) * score_scale
        scores = jnp.where(usable[None, None, :], scores, -jnp.inf)
        row_max = lax.optimization_barrier(jnp.max(scores, axis=2, keepdims=True))
        weights = jnp.exp(scores - row_max)
        weight_sum = lax.optimization_barrier(jnp.sum(weights, axis=2))
        rounded = weights.astype(jnp.bfloat16).astype(jnp.float32)
        mixed = jnp.einsum('hqk,khe->hqe', rounded, values_used, precision=lax.Precision.HIGHEST)
        mixed = mixed / weight_sum[:, :, None]
        return jnp.transpose(mixed, (1, 0, 2)).reshape(patch_rows, D).astype(jnp.bfloat16)
    attended = lax.map(one_patch, jnp.arange(N_PATCH, dtype=jnp.int32)).reshape(TOKENS, D)
    projected = jnp.dot(attended, w_out, preferred_element_type=jnp.float32)
    gate_row = gate_table[timestep[0]].astype(jnp.float32)
    branch = (gate_row[None, :] * projected).astype(jnp.bfloat16)
    next_kv = qkv[:, 1:3, :]
    return (branch, next_kv)
```

```python
import math

import jax
import jax.numpy as jnp
from jax import lax
from jax.experimental import pallas as pl
from jax.experimental.pallas import tpu as pltpu
from jax.sharding import PartitionSpec as P

HEAD_DIM = 128
MASKED = -1e30
VMEM = pl.BlockSpec(memory_space=pltpu.VMEM)
SMEM = pl.BlockSpec(memory_space=pltpu.SMEM)
ANY = pl.BlockSpec(memory_space=pl.ANY)


def params():
    return pltpu.CompilerParams(vmem_limit_bytes=48 * 1024 * 1024)


def ring_order(count):
    return list(range(0, count, 1)) if count < 3 else (
        [0] + list(range(1, count, 2)) + list(range((count - 1) // 2 * 2, 0, -2))
    )


def split_qkv(qkv_t, n_head):
    planes, rows, width = qkv_t.shape
    columns = width // n_head

    def kernel(src, *rest):
        outs, sems = rest[:n_head], rest[n_head]
        mine = lax.axis_index("head")
        copies = []
        for j in range(n_head):
            start = pl.multiple_of((mine ^ j) * columns, columns)
            copies.append(
                pltpu.make_async_copy(src.at[:, :, pl.ds(start, columns)], outs[j], sems.at[j])
            )
        for copy in copies:
            copy.start()
        for copy in copies:
            copy.wait()

    return pl.pallas_call(
        kernel,
        out_shape=[jax.ShapeDtypeStruct((planes, rows, columns), qkv_t.dtype)] * n_head,
        in_specs=[ANY],
        out_specs=[ANY] * n_head,
        scratch_shapes=[pltpu.SemaphoreType.DMA((n_head,))],
        compiler_params=params(),
    )(qkv_t)


def padded(rows):
    return -(-rows // 128) * 128


def weigh(lengths, pieces, stale_keys, origins):
    n_head = len(pieces)
    _, tok_rows, columns = pieces[0].shape
    rows = n_head * tok_rows
    heads = columns // HEAD_DIM
    keep = max(1, rows * 3 // 4)
    per_array = [array.shape[0] // keep for array in stale_keys]
    blocks = sum(per_array)
    pitch = padded(keep)
    total = padded(rows) + blocks * pitch
    scale = 1.0 / math.sqrt(HEAD_DIM)

    def kernel(lengths_ref, *rest):
        piece_refs = rest[:n_head]
        key_refs = rest[n_head : n_head + len(stale_keys)]
        weights_ref, sums_ref, kv_ref, query_buf, key_buf = rest[n_head + len(stale_keys) :]
        mine = lax.axis_index("head")
        patch = lax.axis_index("patch")
        own_limit = lengths_ref[patch]
        position = lax.broadcasted_iota(jnp.int32, (1, tok_rows), 1)
        live_parts = []
        for j in range(n_head):
            here = pl.ds(j * tok_rows, tok_rows)
            query_buf[here, :] = piece_refs[j][0]
            key_buf[here, :] = piece_refs[j][1]
            there = pl.ds(pl.multiple_of((mine ^ j) * tok_rows, tok_rows), tok_rows)
            kv_ref[0, there, :] = piece_refs[j][1]
            kv_ref[1, there, :] = piece_refs[j][2]
        column = lax.broadcasted_iota(jnp.int32, (1, rows), 1)
        absolute = ((column // tok_rows) ^ mine) * tok_rows + column % tok_rows
        fresh_live = absolute < own_limit
        stale_row = lax.broadcasted_iota(jnp.int32, (1, keep), 1)
        limits = origins(lengths_ref, patch)
        for head in range(heads):
            lanes = slice(head * HEAD_DIM, (head + 1) * HEAD_DIM)
            queries = query_buf[:, lanes]

            def score(keys, live):
                found = lax.dot_general(
                    queries, keys, (((1,), (1,)), ((), ())), preferred_element_type=jnp.float32
                )
                return jnp.where(live, found * scale, MASKED)

            parts = [score(key_buf[:, lanes], fresh_live)]
            number = 0
            for ref, count in zip(key_refs, per_array):
                for block in range(count):
                    keys = ref[block * keep : (block + 1) * keep, lanes]
                    parts.append(score(keys, stale_row < limits[number]))
                    number += 1
            top = jnp.max(parts[0], axis=1, keepdims=True)
            for part in parts[1:]:
                top = jnp.maximum(top, jnp.max(part, axis=1, keepdims=True))
            weight_sum = jnp.zeros_like(top)
            for number, part in enumerate(parts):
                weights = jnp.exp(part - top)
                weight_sum = weight_sum + jnp.sum(weights, axis=1, keepdims=True)
                first = 0 if number == 0 else padded(rows) + (number - 1) * pitch
                weights_ref[head, :, first : first + part.shape[1]] = weights.astype(jnp.bfloat16)
            sums_ref[head] = weight_sum

    return pl.pallas_call(
        kernel,
        out_shape=[
            jax.ShapeDtypeStruct((heads, rows, total), jnp.bfloat16),
            jax.ShapeDtypeStruct((heads, rows, 1), jnp.float32),
            jax.ShapeDtypeStruct((2, rows, columns), jnp.bfloat16),
        ],
        in_specs=[SMEM] + [VMEM] * (n_head + len(stale_keys)),
        out_specs=[VMEM] * 3,
        scratch_shapes=[
            pltpu.VMEM((rows, columns), jnp.bfloat16),
            pltpu.VMEM((rows, columns), jnp.bfloat16),
        ],
        compiler_params=params(),
    )(lengths, *pieces, *stale_keys)


def project(weights, sums, pieces, stale_values, w_out, which):
    n_head = len(pieces)
    _, tok_rows, columns = pieces[0].shape
    rows = n_head * tok_rows
    heads = columns // HEAD_DIM
    keep = max(1, rows * 3 // 4)
    per_array = [array.shape[0] // keep for array in stale_values]
    pitch = padded(keep)
    model = w_out.shape[1]
    first_row, row_count = which[0] * tok_rows, len(which) * tok_rows

    def kernel(weights_ref, sums_ref, *rest):
        piece_refs = rest[:n_head]
        value_refs = rest[n_head : n_head + len(stale_values)]
        w_ref = rest[n_head + len(stale_values)]
        out_refs = rest[n_head + len(stale_values) + 1 : -2]
        value_buf, attended_buf = rest[-2:]
        here = slice(first_row, first_row + row_count)
        for j in range(n_head):
            value_buf[j * tok_rows : (j + 1) * tok_rows, :] = piece_refs[j][2]
        for head in range(heads):
            lanes = slice(head * HEAD_DIM, (head + 1) * HEAD_DIM)
            mixed = jnp.dot(
                weights_ref[head, here, :rows],
                value_buf[:, lanes],
                preferred_element_type=jnp.float32,
            )
            first = padded(rows)
            for ref, count in zip(value_refs, per_array):
                for block in range(count):
                    mixed = mixed + jnp.dot(
                        weights_ref[head, here, first : first + keep],
                        ref[block * keep : (block + 1) * keep, lanes],
                        preferred_element_type=jnp.float32,
                    )
                    first += pitch
            attended_buf[:, lanes] = (mixed / sums_ref[head, here, :]).astype(jnp.bfloat16)
        result = jnp.dot(attended_buf[...], w_ref[...], preferred_element_type=jnp.float32)
        for number, ref in enumerate(out_refs):
            ref[...] = result[number * tok_rows : (number + 1) * tok_rows].astype(ref.dtype)

    return pl.pallas_call(
        kernel,
        out_shape=[jax.ShapeDtypeStruct((tok_rows, model), jnp.bfloat16)] * len(which),
        in_specs=[VMEM] * (3 + n_head + len(stale_values)),
        out_specs=[VMEM] * len(which),
        scratch_shapes=[
            pltpu.VMEM((rows, columns), jnp.bfloat16),
            pltpu.VMEM((row_count, columns), jnp.bfloat16),
        ],
        compiler_params=params(),
    )(weights, sums, *pieces, *stale_values, w_out)


def add_pair(left, right):
    return (left.astype(jnp.float32) + right.astype(jnp.float32)).astype(jnp.bfloat16)


def build(n_head, n_patch):
    flip = [[(i, i ^ j) for i in range(n_head)] for j in range(n_head)]
    order = ring_order(n_patch)
    ring = [(order[i], order[(i + 1) % n_patch]) for i in range(n_patch)]
    on_line = n_patch <= 4

    def ring_limits(lengths_ref, patch):
        place = sum(jnp.where(patch == order[i], i, 0) for i in range(n_patch))
        limits = []
        for step in range(1, n_patch):
            back = lax.rem(place + n_patch - step, n_patch)
            origin = sum(jnp.where(back == i, order[i], 0) for i in range(n_patch))
            limits.append(lengths_ref[origin])
        return limits

    def gathered_limits(lengths_ref, patch):
        return [jnp.where(patch == i, 0, lengths_ref[i]) for i in range(n_patch)]

    def shards(qkv, stale_kv, w_out, gate_table, lengths, timestep):
        patch_rows = stale_kv.shape[0]
        keep = patch_rows * 3 // 4
        stale_k, stale_v = stale_kv[:keep, 0], stale_kv[:keep, 1]
        if on_line:
            keys, values = [stale_k], [stale_v]
            for _ in range(n_patch - 1):
                keys.append(lax.ppermute(keys[-1], "patch", ring))
                values.append(lax.ppermute(values[-1], "patch", ring))
            keys, values, origins = keys[1:], values[1:], ring_limits
        else:
            keys = [lax.all_gather(stale_k, "patch", axis=0, tiled=True)]
            values = [lax.all_gather(stale_v, "patch", axis=0, tiled=True)]
            origins = gathered_limits
        sent = split_qkv(jnp.transpose(qkv, (1, 0, 2)), n_head)
        pieces = [sent[0]] + [lax.ppermute(sent[j], "head", flip[j]) for j in range(1, n_head)]
        weights, sums, next_t = weigh(lengths, pieces, keys, origins)
        next_kv = jnp.transpose(next_t, (1, 0, 2))

        half = n_head // 2
        far = project(weights, sums, pieces, values, w_out, range(half, n_head))
        near = project(weights, sums, pieces, values, w_out, range(0, half))
        held = list(near) + list(far)
        bit = 1
        while bit < n_head:
            merged = [None] * n_head
            for j in reversed(range(n_head)):
                if j % (2 * bit) == 0:
                    arrived = lax.ppermute(held[j + bit], "head", flip[bit])
                    if 2 * bit < n_head:
                        merged[j] = add_pair(held[j], arrived)
                    else:
                        merged[j] = held[j].astype(jnp.float32) + arrived.astype(jnp.float32)
            held = merged
            bit *= 2
        projected = held[0].astype(jnp.float32)
        gate_row = lax.dynamic_slice_in_dim(gate_table, timestep[0], 1, 0)[0].astype(jnp.float32)
        branch = (gate_row[None, :] * projected).astype(jnp.bfloat16)
        return (branch, next_kv)

    return shards


def solution(mesh):
    return jax.shard_map(
        build(mesh.shape["head"], mesh.shape["patch"]),
        mesh=mesh,
        in_specs=(
            P(("groups", "patch", "head"), None, None),
            P(("groups", "patch"), None, "head"),
            P("head", None),
            P(),
            P("groups"),
            P("groups"),
        ),
        out_specs=(P(("groups", "patch", "head"), None), P(("groups", "patch"), None, "head")),
        check_vma=False,
    )
```

```python
import math

import jax
import jax.numpy as jnp
from jax import lax
from jax.experimental import pallas as pl
from jax.experimental.pallas import tpu as pltpu
from jax.sharding import PartitionSpec as P

HEAD_DIM = 128
MASKED = -1e30
VMEM = pl.BlockSpec(memory_space=pltpu.VMEM)
SMEM = pl.BlockSpec(memory_space=pltpu.SMEM)
ANY = pl.BlockSpec(memory_space=pl.ANY)


MIB = 1024 * 1024
SPLIT_ROOM, WEIGH_ROOM, PROJECT_ROOM = 8 * MIB, 46 * MIB, 32 * MIB


def params(room):
    return pltpu.CompilerParams(vmem_limit_bytes=room)


def padded(rows):
    return -(-rows // 128) * 128


def split_qkv(qkv_t, lengths, n_head, keep, origins):
    planes, tok_rows, width = qkv_t.shape
    columns = width // n_head
    rows = n_head * tok_rows
    pitch = padded(keep)
    blocks = len(origins(None, None))
    total = padded(rows) + blocks * pitch

    def kernel(src, lengths_ref, *rest):
        outs, live_ref, sems = rest[:n_head], rest[n_head], rest[n_head + 1]
        mine = lax.axis_index("head")
        patch = lax.axis_index("patch")
        copies = []
        for j in range(n_head):
            start = pl.multiple_of((mine ^ j) * columns, columns)
            copies.append(
                pltpu.make_async_copy(src.at[:, :, pl.ds(start, columns)], outs[j], sems.at[j])
            )
        for copy in copies:
            copy.start()
        column = lax.broadcasted_iota(jnp.int32, (8, padded(rows)), 1)
        absolute = ((column // tok_rows) ^ mine) * tok_rows + column % tok_rows
        live_ref[:, : padded(rows)] = jnp.where(
            (absolute < lengths_ref[patch]) & (column < rows), 1.0, 0.0
        )
        row = lax.broadcasted_iota(jnp.int32, (8, pitch), 1)
        for number, limit in enumerate(origins(lengths_ref, patch)):
            first = padded(rows) + number * pitch
            live_ref[:, first : first + pitch] = jnp.where(row < limit, 1.0, 0.0)
        for copy in copies:
            copy.wait()

    return pl.pallas_call(
        kernel,
        out_shape=[jax.ShapeDtypeStruct((planes, tok_rows, columns), qkv_t.dtype)] * n_head
        + [jax.ShapeDtypeStruct((8, total), jnp.float32)],
        in_specs=[ANY, SMEM],
        out_specs=[ANY] * n_head + [VMEM],
        scratch_shapes=[pltpu.SemaphoreType.DMA((n_head,))],
        compiler_params=params(SPLIT_ROOM),
    )(qkv_t, lengths)


def weigh(live, pieces, stale_keys, w_out):
    n_head = len(pieces)
    _, tok_rows, columns = pieces[0].shape
    rows = n_head * tok_rows
    heads = columns // HEAD_DIM
    keep = rows * 3 // 4
    per_array = [array.shape[1] // keep for array, _ in stale_keys]
    pitch = padded(keep)
    total = live.shape[1]
    scale = 1.0 / math.sqrt(HEAD_DIM)

    def kernel(live_ref, *rest):
        piece_refs = rest[:n_head]
        key_refs = rest[n_head : n_head + len(stale_keys)]
        rest = rest[n_head + len(stale_keys) :]
        w_ref, weights_ref, sums_ref, kv_ref, held_ref, query_buf, key_buf, sem = rest
        bring = pltpu.make_async_copy(w_ref, held_ref, sem)
        bring.start()
        mine = lax.axis_index("head")
        for j in range(n_head):
            here = pl.ds(j * tok_rows, tok_rows)
            query_buf[here, :] = piece_refs[j][0]
            key_buf[here, :] = piece_refs[j][1]
            there = pl.ds(pl.multiple_of((mine ^ j) * tok_rows, tok_rows), tok_rows)
            kv_ref[0, there, :] = piece_refs[j][1]
            kv_ref[1, there, :] = piece_refs[j][2]
        for head in range(heads):
            lanes = slice(head * HEAD_DIM, (head + 1) * HEAD_DIM)
            queries = query_buf[:, lanes]

            def score(keys, first):
                found = lax.dot_general(
                    queries, keys, (((1,), (1,)), ((), ())), preferred_element_type=jnp.float32
                )
                usable = live_ref[0:1, first : first + keys.shape[0]] > 0.5
                return jnp.where(usable, found * scale, MASKED)

            parts, firsts = [score(key_buf[:, lanes], 0)], [0]
            first = padded(rows)
            for ref, (_, plane), count in zip(key_refs, stale_keys, per_array):
                for block in range(count):
                    keys = ref[plane, block * keep : (block + 1) * keep, lanes]
                    parts.append(score(keys, first))
                    firsts.append(first)
                    first += pitch
            top = jnp.max(parts[0], axis=1, keepdims=True)
            for part in parts[1:]:
                top = jnp.maximum(top, jnp.max(part, axis=1, keepdims=True))
            weight_sum = jnp.zeros_like(top)
            for part, first in zip(parts, firsts):
                weights = jnp.exp(part - top)
                weight_sum = weight_sum + jnp.sum(weights, axis=1, keepdims=True)
                weights_ref[head, :, first : first + part.shape[1]] = weights.astype(jnp.bfloat16)
            sums_ref[head] = weight_sum
        bring.wait()

    return pl.pallas_call(
        kernel,
        out_shape=[
            jax.ShapeDtypeStruct((heads, rows, total), jnp.bfloat16),
            jax.ShapeDtypeStruct((heads, rows, 1), jnp.float32),
            jax.ShapeDtypeStruct((2, rows, columns), jnp.bfloat16),
            jax.ShapeDtypeStruct(w_out.shape, w_out.dtype),
        ],
        in_specs=[VMEM] * (1 + n_head + len(stale_keys)) + [ANY],
        out_specs=[VMEM] * 4,
        scratch_shapes=[
            pltpu.VMEM((rows, columns), jnp.bfloat16),
            pltpu.VMEM((rows, columns), jnp.bfloat16),
            pltpu.SemaphoreType.DMA,
        ],
        compiler_params=params(WEIGH_ROOM),
    )(live, *pieces, *[array for array, _ in stale_keys], w_out)


def project(weights, sums, pieces, stale_values, w_out, which):
    n_head = len(pieces)
    _, tok_rows, columns = pieces[0].shape
    rows = n_head * tok_rows
    heads = columns // HEAD_DIM
    keep = rows * 3 // 4
    per_array = [array.shape[1] // keep for array, _ in stale_values]
    pitch = padded(keep)
    model = w_out.shape[1]
    first_row, row_count = which[0] * tok_rows, len(which) * tok_rows

    def kernel(weights_ref, sums_ref, *rest):
        piece_refs = rest[:n_head]
        value_refs = rest[n_head : n_head + len(stale_values)]
        w_ref = rest[n_head + len(stale_values)]
        out_refs = rest[n_head + len(stale_values) + 1 : -2]
        value_buf, attended_buf = rest[-2:]
        here = slice(first_row, first_row + row_count)
        for j in range(n_head):
            value_buf[j * tok_rows : (j + 1) * tok_rows, :] = piece_refs[j][2]
        for head in range(heads):
            lanes = slice(head * HEAD_DIM, (head + 1) * HEAD_DIM)
            mixed = jnp.dot(
                weights_ref[head, here, :rows],
                value_buf[:, lanes],
                preferred_element_type=jnp.float32,
            )
            first = padded(rows)
            for ref, (_, plane), count in zip(value_refs, stale_values, per_array):
                for block in range(count):
                    mixed = mixed + jnp.dot(
                        weights_ref[head, here, first : first + keep],
                        ref[plane, block * keep : (block + 1) * keep, lanes],
                        preferred_element_type=jnp.float32,
                    )
                    first += pitch
            attended_buf[:, lanes] = (mixed / sums_ref[head, here, :]).astype(jnp.bfloat16)
        result = jnp.dot(attended_buf[...], w_ref[...], preferred_element_type=jnp.float32)
        for number, ref in enumerate(out_refs):
            ref[...] = result[number * tok_rows : (number + 1) * tok_rows].astype(ref.dtype)

    return pl.pallas_call(
        kernel,
        out_shape=[jax.ShapeDtypeStruct((tok_rows, model), jnp.bfloat16)] * len(which),
        in_specs=[VMEM] * (3 + n_head + len(stale_values)),
        out_specs=[VMEM] * len(which),
        scratch_shapes=[
            pltpu.VMEM((rows, columns), jnp.bfloat16),
            pltpu.VMEM((row_count, columns), jnp.bfloat16),
        ],
        compiler_params=params(PROJECT_ROOM),
    )(weights, sums, *pieces, *[array for array, _ in stale_values], w_out)


def add_pair(left, right):
    return (left.astype(jnp.float32) + right.astype(jnp.float32)).astype(jnp.bfloat16)


def build(n_head, n_patch):
    flip = [[(i, i ^ j) for i in range(n_head)] for j in range(n_head)]
    order = [0, 1, 3, 2]
    on_ring = n_patch == len(order)
    onward = [(order[i], order[(i + 1) % len(order)]) for i in range(len(order))]
    backward = [(b, a) for a, b in onward]

    def ring_limits(lengths_ref, patch):
        limits = []
        for back in (1, 3, 2):
            if lengths_ref is None:
                limits.append(None)
                continue
            origin = sum(jnp.where(patch == order[i], order[i - back], 0) for i in range(4))
            limits.append(lengths_ref[origin])
        return limits

    def gathered_limits(lengths_ref, patch):
        if lengths_ref is None:
            return [None] * n_patch
        return [jnp.where(patch == i, 0, lengths_ref[i]) for i in range(n_patch)]

    def shards(qkv, stale_kv, w_out, gate_table, lengths, timestep):
        keep = stale_kv.shape[0] * 3 // 4
        origins = ring_limits if on_ring else gathered_limits
        qkv_t = jnp.transpose(qkv, (1, 0, 2))
        *sent, live = split_qkv(qkv_t, lengths, n_head, keep, origins)
        stale = jnp.transpose(stale_kv[:keep], (1, 0, 2))
        if on_ring:
            key_before = lax.ppermute(stale[:1], "patch", onward)
            stale, live = lax.optimization_barrier((stale, live))
            value_before = lax.ppermute(stale[1:], "patch", onward)
            after = lax.ppermute(stale, "patch", backward)
            key_two = lax.ppermute(key_before, "patch", onward)
            value_two = lax.ppermute(value_before, "patch", onward)
            keys = [(key_before, 0), (after, 0), (key_two, 0)]
            values = [(value_before, 0), (after, 1), (value_two, 0)]
        else:
            gathered = lax.all_gather(stale, "patch", axis=1, tiled=True)
            keys, values = [(gathered, 0)], [(gathered, 1)]
        pieces = [sent[0]] + [lax.ppermute(sent[j], "head", flip[j]) for j in range(1, n_head)]
        weights, sums, next_t, w_held = weigh(live, pieces, keys, w_out)
        next_kv = jnp.transpose(next_t, (1, 0, 2))
        gate_row = lax.dynamic_slice_in_dim(gate_table, timestep[0], 1, 0)[0].astype(jnp.float32)

        def combine(held):
            bit = 1
            while len(held) > 1:
                arrived = [lax.ppermute(held[j], "head", flip[bit]) for j in range(1, len(held), 2)]
                held = [add_pair(held[2 * i], arrived[i]) for i in range(len(arrived))]
                bit *= 2
            return held[0]

        half = n_head // 2
        partial = project(weights, sums, pieces, values, w_held, range(n_head))
        arrived = lax.ppermute(combine(partial[half:]), "head", flip[half])
        near = combine(partial[:half])
        projected = near.astype(jnp.float32) + arrived.astype(jnp.float32)
        branch = (gate_row[None, :] * projected).astype(jnp.bfloat16)
        return (branch, next_kv)

    return shards


def solution(mesh):
    return jax.shard_map(
        build(mesh.shape["head"], mesh.shape["patch"]),
        mesh=mesh,
        in_specs=(
            P(("groups", "patch", "head"), None, None),
            P(("groups", "patch"), None, "head"),
            P("head", None),
            P(),
            P("groups"),
            P("groups"),
        ),
        out_specs=(P(("groups", "patch", "head"), None), P(("groups", "patch"), None, "head")),
        check_vma=False,
    )
```

```python
import math

import jax
import jax.numpy as jnp
from jax import lax
from jax.experimental import pallas as pl
from jax.experimental.pallas import tpu as pltpu
from jax.sharding import PartitionSpec as P

HEAD_DIM = 128
MASKED = -1e30
VMEM = pl.BlockSpec(memory_space=pltpu.VMEM)
SMEM = pl.BlockSpec(memory_space=pltpu.SMEM)
ANY = pl.BlockSpec(memory_space=pl.ANY)


MIB = 1024 * 1024
SPLIT_ROOM, WEIGH_ROOM, PROJECT_ROOM = 8 * MIB, 46 * MIB, 32 * MIB


def params(room):
    return pltpu.CompilerParams(vmem_limit_bytes=room)


def padded(rows):
    return -(-rows // 128) * 128


def split_qkv(qkv_t, n_head):
    planes, tok_rows, width = qkv_t.shape
    columns = width // n_head

    def kernel(src, *rest):
        outs, sems = rest[:n_head], rest[n_head]
        mine = lax.axis_index("head")
        copies = []
        for j in range(n_head):
            start = pl.multiple_of((mine ^ j) * columns, columns)
            copies.append(
                pltpu.make_async_copy(src.at[:, :, pl.ds(start, columns)], outs[j], sems.at[j])
            )
        for copy in copies:
            copy.start()
        for copy in copies:
            copy.wait()

    return pl.pallas_call(
        kernel,
        out_shape=[jax.ShapeDtypeStruct((planes, tok_rows, columns), qkv_t.dtype)] * n_head,
        in_specs=[ANY],
        out_specs=[ANY] * n_head,
        scratch_shapes=[pltpu.SemaphoreType.DMA((n_head,))],
        compiler_params=params(SPLIT_ROOM),
    )(qkv_t)


def weigh(live, pieces, stale_keys, w_out):
    n_head = len(pieces)
    _, tok_rows, columns = pieces[0].shape
    rows = n_head * tok_rows
    heads = columns // HEAD_DIM
    keep = rows * 3 // 4
    per_array = [array.shape[1] // keep for array, _ in stale_keys]
    pitch = padded(keep)
    total = live.shape[1]
    scale = 1.0 / math.sqrt(HEAD_DIM)

    def kernel(live_ref, *rest):
        piece_refs = rest[:n_head]
        key_refs = rest[n_head : n_head + len(stale_keys)]
        rest = rest[n_head + len(stale_keys) :]
        w_ref, weights_ref, sums_ref, kv_ref, held_ref, query_buf, key_buf, sem = rest
        bring = pltpu.make_async_copy(w_ref, held_ref, sem)
        bring.start()
        mine = lax.axis_index("head")
        for j in range(n_head):
            here = pl.ds(j * tok_rows, tok_rows)
            query_buf[here, :] = piece_refs[j][0]
            key_buf[here, :] = piece_refs[j][1]
            there = pl.ds(pl.multiple_of((mine ^ j) * tok_rows, tok_rows), tok_rows)
            kv_ref[0, there, :] = piece_refs[j][1]
            kv_ref[1, there, :] = piece_refs[j][2]
        for head in range(heads):
            lanes = slice(head * HEAD_DIM, (head + 1) * HEAD_DIM)
            queries = query_buf[:, lanes]

            def score(keys, first):
                found = lax.dot_general(
                    queries, keys, (((1,), (1,)), ((), ())), preferred_element_type=jnp.float32
                )
                usable = live_ref[0:1, first : first + keys.shape[0]] > 0
                return jnp.where(usable, found * scale, MASKED)

            parts, firsts = [score(key_buf[:, lanes], 0)], [0]
            first = padded(rows)
            for ref, (_, plane), count in zip(key_refs, stale_keys, per_array):
                for block in range(count):
                    keys = ref[plane, block * keep : (block + 1) * keep, lanes]
                    parts.append(score(keys, first))
                    firsts.append(first)
                    first += pitch
            top = jnp.max(parts[0], axis=1, keepdims=True)
            for part in parts[1:]:
                top = jnp.maximum(top, jnp.max(part, axis=1, keepdims=True))
            weight_sum = jnp.zeros_like(top)
            for part, first in zip(parts, firsts):
                weights = jnp.exp(part - top)
                weight_sum = weight_sum + jnp.sum(weights, axis=1, keepdims=True)
                weights_ref[head, :, first : first + part.shape[1]] = weights.astype(jnp.bfloat16)
            sums_ref[head] = weight_sum
        bring.wait()

    return pl.pallas_call(
        kernel,
        out_shape=[
            jax.ShapeDtypeStruct((heads, rows, total), jnp.bfloat16),
            jax.ShapeDtypeStruct((heads, rows, 1), jnp.float32),
            jax.ShapeDtypeStruct((2, rows, columns), jnp.bfloat16),
            jax.ShapeDtypeStruct(w_out.shape, w_out.dtype),
        ],
        in_specs=[VMEM] * (1 + n_head + len(stale_keys)) + [ANY],
        out_specs=[VMEM] * 4,
        scratch_shapes=[
            pltpu.VMEM((rows, columns), jnp.bfloat16),
            pltpu.VMEM((rows, columns), jnp.bfloat16),
            pltpu.SemaphoreType.DMA,
        ],
        compiler_params=params(WEIGH_ROOM),
    )(live, *pieces, *[array for array, _ in stale_keys], w_out)


def project(weights, sums, pieces, stale_values, w_out, which):
    n_head = len(pieces)
    _, tok_rows, columns = pieces[0].shape
    rows = n_head * tok_rows
    heads = columns // HEAD_DIM
    keep = rows * 3 // 4
    per_array = [array.shape[1] // keep for array, _ in stale_values]
    pitch = padded(keep)
    model = w_out.shape[1]
    first_row, row_count = which[0] * tok_rows, len(which) * tok_rows

    def kernel(weights_ref, sums_ref, *rest):
        piece_refs = rest[:n_head]
        value_refs = rest[n_head : n_head + len(stale_values)]
        w_ref = rest[n_head + len(stale_values)]
        out_refs = rest[n_head + len(stale_values) + 1 : -2]
        value_buf, attended_buf = rest[-2:]
        here = slice(first_row, first_row + row_count)
        for j in range(n_head):
            value_buf[j * tok_rows : (j + 1) * tok_rows, :] = piece_refs[j][2]
        for head in range(heads):
            lanes = slice(head * HEAD_DIM, (head + 1) * HEAD_DIM)
            mixed = jnp.dot(
                weights_ref[head, here, :rows],
                value_buf[:, lanes],
                preferred_element_type=jnp.float32,
            )
            first = padded(rows)
            for ref, (_, plane), count in zip(value_refs, stale_values, per_array):
                for block in range(count):
                    mixed = mixed + jnp.dot(
                        weights_ref[head, here, first : first + keep],
                        ref[plane, block * keep : (block + 1) * keep, lanes],
                        preferred_element_type=jnp.float32,
                    )
                    first += pitch
            attended_buf[:, lanes] = (mixed / sums_ref[head, here, :]).astype(jnp.bfloat16)
        result = jnp.dot(attended_buf[...], w_ref[...], preferred_element_type=jnp.float32)
        for number, ref in enumerate(out_refs):
            ref[...] = result[number * tok_rows : (number + 1) * tok_rows].astype(ref.dtype)

    return pl.pallas_call(
        kernel,
        out_shape=[jax.ShapeDtypeStruct((tok_rows, model), jnp.bfloat16)] * len(which),
        in_specs=[VMEM] * (3 + n_head + len(stale_values)),
        out_specs=[VMEM] * len(which),
        scratch_shapes=[
            pltpu.VMEM((rows, columns), jnp.bfloat16),
            pltpu.VMEM((row_count, columns), jnp.bfloat16),
        ],
        compiler_params=params(PROJECT_ROOM),
    )(weights, sums, *pieces, *[array for array, _ in stale_values], w_out)


def add_pair(left, right):
    return (left.astype(jnp.float32) + right.astype(jnp.float32)).astype(jnp.bfloat16)


def build(n_head, n_patch):
    flip = [[(i, i ^ j) for i in range(n_head)] for j in range(n_head)]
    order = [0, 1, 3, 2]
    on_ring = n_patch == len(order)
    onward = [(order[i], order[(i + 1) % len(order)]) for i in range(len(order))]
    backward = [(b, a) for a, b in onward]

    if on_ring:
        sources = [[order[order.index(p) - back] for back in (1, 3, 2)] for p in range(n_patch)]
    else:
        sources = [[q if q != p else n_patch for q in range(n_patch)] for p in range(n_patch)]

    def mark_live(lengths, tok_rows, keep):
        rows, pitch = n_head * tok_rows, padded(keep)
        owner, within = [], []
        for p in range(n_patch):
            owner.append([p] * rows + [n_patch] * (padded(rows) - rows))
            for source in sources[p]:
                owner[p] += [source] * keep + [n_patch] * (pitch - keep)
        total = len(owner[0])
        column = lax.broadcasted_iota(jnp.int32, (1, total), 1)
        mine = lax.axis_index("head").astype(jnp.int32)
        own = lax.dynamic_slice(
            jnp.asarray(owner, jnp.int32),
            (lax.axis_index("patch").astype(jnp.uint32), jnp.uint32(0)),
            (1, total),
        )
        fresh = column ^ (mine * tok_rows)
        within = jnp.where(column < padded(rows), fresh, (column - padded(rows)) % pitch)
        patches = lax.broadcasted_iota(jnp.int32, (n_patch, total), 0)
        found = (own == patches) & (within < lengths[:, None])
        return jnp.sum(found.astype(jnp.int32), axis=0, keepdims=True)

    def shards(qkv, stale_kv, w_out, gate_table, lengths, timestep):
        keep = stale_kv.shape[0] * 3 // 4
        qkv_t = jnp.transpose(qkv, (1, 0, 2))
        stale = jnp.transpose(stale_kv[:keep], (1, 0, 2))
        stale, qkv_t = lax.optimization_barrier((stale, qkv_t))
        sent = split_qkv(qkv_t, n_head)
        live = mark_live(lengths, qkv.shape[0], keep)
        if on_ring:
            key_before = lax.ppermute(stale[:1], "patch", onward)
            key_before, _ = lax.optimization_barrier((key_before, sent[0]))
            value_before = lax.ppermute(stale[1:], "patch", onward)
            after = lax.ppermute(stale, "patch", backward)
            key_two = lax.ppermute(key_before, "patch", onward)
            value_two = lax.ppermute(value_before, "patch", onward)
            keys = [(key_before, 0), (after, 0), (key_two, 0)]
            values = [(value_before, 0), (after, 1), (value_two, 0)]
        else:
            gathered = lax.all_gather(stale, "patch", axis=1, tiled=True)
            keys, values = [(gathered, 0)], [(gathered, 1)]
        pieces = [sent[0]] + [lax.ppermute(sent[j], "head", flip[j]) for j in range(1, n_head)]
        weights, sums, next_t, w_held = weigh(live, pieces, keys, w_out)
        next_kv = jnp.transpose(next_t, (1, 0, 2))
        steps = lax.broadcasted_iota(jnp.int32, gate_table.shape, 0)
        gate_row = jnp.sum(
            jnp.where(steps == timestep[:, None], gate_table.astype(jnp.float32), 0.0), axis=0
        )

        def combine(held):
            bit = 1
            while len(held) > 1:
                arrived = [lax.ppermute(held[j], "head", flip[bit]) for j in range(1, len(held), 2)]
                held = [add_pair(held[2 * i], arrived[i]) for i in range(len(arrived))]
                bit *= 2
            return held[0]

        half = n_head // 2
        partial = project(weights, sums, pieces, values, w_held, range(n_head))
        arrived = lax.ppermute(combine(partial[half:]), "head", flip[half])
        near = combine(partial[:half])
        projected = near.astype(jnp.float32) + arrived.astype(jnp.float32)
        branch = (gate_row[None, :] * projected).astype(jnp.bfloat16)
        return (branch, next_kv)

    return shards


def solution(mesh):
    return jax.shard_map(
        build(mesh.shape["head"], mesh.shape["patch"]),
        mesh=mesh,
        in_specs=(
            P(("groups", "patch", "head"), None, None),
            P(("groups", "patch"), None, "head"),
            P("head", None),
            P(),
            P("groups"),
            P("groups"),
        ),
        out_specs=(P(("groups", "patch", "head"), None), P(("groups", "patch"), None, "head")),
        check_vma=False,
    )
```

```python
import math

import jax
import jax.numpy as jnp
from jax import lax
from jax.experimental import pallas as pl
from jax.experimental.pallas import tpu as pltpu
from jax.sharding import PartitionSpec as P

HEAD_DIM = 128
MASKED = -1e30
VMEM = pl.BlockSpec(memory_space=pltpu.VMEM)
SMEM = pl.BlockSpec(memory_space=pltpu.SMEM)
ANY = pl.BlockSpec(memory_space=pl.ANY)


MIB = 1024 * 1024
SPLIT_ROOM, WEIGH_ROOM, PROJECT_ROOM = 8 * MIB, 46 * MIB, 32 * MIB

HALVES = 2


def params(room):
    return pltpu.CompilerParams(vmem_limit_bytes=room)


def padded(rows):
    return -(-rows // 128) * 128


def split_qkv(qkv_t, n_head):
    planes, tok_rows, width = qkv_t.shape
    columns = width // n_head

    def kernel(src, *rest):
        outs, sems = rest[:n_head], rest[n_head]
        mine = lax.axis_index("head")
        copies = []
        for j in range(n_head):
            start = pl.multiple_of((mine ^ j) * columns, columns)
            copies.append(
                pltpu.make_async_copy(src.at[:, :, pl.ds(start, columns)], outs[j], sems.at[j])
            )
        for copy in copies:
            copy.start()
        for copy in copies:
            copy.wait()

    return pl.pallas_call(
        kernel,
        out_shape=[jax.ShapeDtypeStruct((planes, tok_rows, columns), qkv_t.dtype)] * n_head,
        in_specs=[ANY],
        out_specs=[ANY] * n_head,
        scratch_shapes=[pltpu.SemaphoreType.DMA((n_head,))],
        compiler_params=params(SPLIT_ROOM),
    )(qkv_t)


def weigh(live, pieces, stale_keys, early_values, w_out):
    n_head = len(pieces)
    _, tok_rows, columns = pieces[0].shape
    rows = n_head * tok_rows
    heads = columns // HEAD_DIM
    keep = rows * 3 // 4
    pitch = padded(keep)
    n_keys, n_values = len(stale_keys), len(early_values)
    per_array = [array.shape[1] // keep for array, _ in stale_keys]
    late_blocks = sum(per_array[n_values:])
    scale = 1.0 / math.sqrt(HEAD_DIM)

    def kernel(live_ref, *rest):
        piece_refs, rest = rest[:n_head], rest[n_head:]
        key_refs, rest = rest[:n_keys], rest[n_keys:]
        value_refs, rest = rest[:n_values], rest[n_values:]
        w_ref, weights_ref, mixed_ref, sums_ref, kv_ref, held_ref, *rest = rest
        query_buf, key_buf, value_buf, sem = rest
        bring = pltpu.make_async_copy(w_ref, held_ref, sem)
        bring.start()
        mine = lax.axis_index("head")
        for j in range(n_head):
            here = pl.ds(j * tok_rows, tok_rows)
            query_buf[here, :] = piece_refs[j][0]
            key_buf[here, :] = piece_refs[j][1]
            value_buf[here, :] = piece_refs[j][2]
            there = pl.ds(pl.multiple_of((mine ^ j) * tok_rows, tok_rows), tok_rows)
            kv_ref[0, there, :] = piece_refs[j][1]
            kv_ref[1, there, :] = piece_refs[j][2]
        for head in range(heads):
            lanes = slice(head * HEAD_DIM, (head + 1) * HEAD_DIM)
            queries = query_buf[:, lanes]

            def score(keys, first):
                found = lax.dot_general(
                    queries, keys, (((1,), (1,)), ((), ())), preferred_element_type=jnp.float32
                )
                usable = live_ref[0:1, first : first + keys.shape[0]] > 0
                return jnp.where(usable, found * scale, MASKED)

            parts, values = [score(key_buf[:, lanes], 0)], [value_buf[:, lanes]]
            first = padded(rows)
            for number, (_, plane) in enumerate(stale_keys):
                for block in range(per_array[number]):
                    slots = slice(block * keep, (block + 1) * keep)
                    parts.append(score(key_refs[number][plane, slots, lanes], first))
                    first += pitch
                    if number < n_values:
                        values.append(value_refs[number][early_values[number][1], slots, lanes])
            top = jnp.max(parts[0], axis=1, keepdims=True)
            for part in parts[1:]:
                top = jnp.maximum(top, jnp.max(part, axis=1, keepdims=True))
            weight_sum = jnp.zeros_like(top)
            mixed = jnp.zeros((rows, HEAD_DIM), jnp.float32)
            for number, part in enumerate(parts):
                weights = jnp.exp(part - top)
                weight_sum = weight_sum + jnp.sum(weights, axis=1, keepdims=True)
                rounded = weights.astype(jnp.bfloat16)
                if number < len(values):
                    mixed = mixed + jnp.dot(
                        rounded, values[number], preferred_element_type=jnp.float32
                    )
                else:
                    first = (number - len(values)) * pitch
                    weights_ref[head, :, first : first + keep] = rounded
            mixed_ref[:, lanes] = mixed
            sums_ref[head] = weight_sum
        bring.wait()

    return pl.pallas_call(
        kernel,
        out_shape=[
            jax.ShapeDtypeStruct((heads, rows, late_blocks * pitch), jnp.bfloat16),
            jax.ShapeDtypeStruct((rows, columns), jnp.float32),
            jax.ShapeDtypeStruct((heads, rows, 1), jnp.float32),
            jax.ShapeDtypeStruct((2, rows, columns), jnp.bfloat16),
            jax.ShapeDtypeStruct(w_out.shape, w_out.dtype),
        ],
        in_specs=[VMEM] * (1 + n_head + n_keys + n_values) + [ANY],
        out_specs=[VMEM] * 5,
        scratch_shapes=[pltpu.VMEM((rows, columns), jnp.bfloat16)] * 3
        + [pltpu.SemaphoreType.DMA],
        compiler_params=params(WEIGH_ROOM),
    )(
        live,
        *pieces,
        *[array for array, _ in stale_keys],
        *[array for array, _ in early_values],
        w_out,
    )


def project(weights, mixed, sums, late_values, w_out, cuts):
    rows, columns = mixed.shape
    heads = columns // HEAD_DIM
    keep = rows * 3 // 4
    pitch = padded(keep)
    model = w_out.shape[1]
    n_values = len(late_values)

    def kernel(weights_ref, mixed_ref, sums_ref, *rest):
        value_refs, w_ref, out_refs = rest[:n_values], rest[n_values], rest[n_values + 1 : -1]
        attended_buf = rest[-1]
        for head in range(heads):
            lanes = slice(head * HEAD_DIM, (head + 1) * HEAD_DIM)
            total = mixed_ref[:, lanes]
            first = 0
            for ref, (array, plane) in zip(value_refs, late_values):
                for block in range(array.shape[1] // keep):
                    total = total + jnp.dot(
                        weights_ref[head, :, first : first + keep],
                        ref[plane, block * keep : (block + 1) * keep, lanes],
                        preferred_element_type=jnp.float32,
                    )
                    first += pitch
            attended_buf[:, lanes] = (total / sums_ref[head]).astype(jnp.bfloat16)
        result = jnp.dot(attended_buf[...], w_ref[...], preferred_element_type=jnp.float32)
        for (start, stop), ref in zip(cuts, out_refs):
            ref[...] = result[start:stop].astype(ref.dtype)

    return pl.pallas_call(
        kernel,
        out_shape=[jax.ShapeDtypeStruct((stop - start, model), jnp.bfloat16) for start, stop in cuts],
        in_specs=[VMEM] * (4 + n_values),
        out_specs=[VMEM] * len(cuts),
        scratch_shapes=[pltpu.VMEM((rows, columns), jnp.bfloat16)],
        compiler_params=params(PROJECT_ROOM),
    )(weights, mixed, sums, *[array for array, _ in late_values], w_out)


def finish(near, arrived, gate_row):
    def kernel(gate_ref, *rest):
        near_refs, arrived_refs, out_ref = rest[: len(near)], rest[len(near) : -1], rest[-1]
        start = 0
        for ref in arrived_refs:
            here = slice(start, start + ref.shape[0])
            total = ref[...].astype(jnp.float32)
            for near_ref in near_refs:
                total = total + near_ref[here].astype(jnp.float32)
            out_ref[here] = (gate_ref[...] * total).astype(out_ref.dtype)
            start += ref.shape[0]

    return pl.pallas_call(
        kernel,
        out_shape=jax.ShapeDtypeStruct(near[0].shape, near[0].dtype),
        in_specs=[VMEM] * (1 + len(near) + len(arrived)),
        out_specs=VMEM,
        compiler_params=params(PROJECT_ROOM),
    )(gate_row, *near, *arrived)


def add_pair(left, right):
    return (left.astype(jnp.float32) + right.astype(jnp.float32)).astype(jnp.bfloat16)


def build(n_head, n_patch):
    flip = [[(i, i ^ j) for i in range(n_head)] for j in range(n_head)]
    order = [0, 1, 3, 2]
    on_ring = n_patch == len(order)
    onward = [(order[i], order[(i + 1) % len(order)]) for i in range(len(order))]
    backward = [(b, a) for a, b in onward]

    if on_ring:
        sources = [[order[order.index(p) - back] for back in (1, 3, 2)] for p in range(n_patch)]
    else:
        sources = [[q if q != p else n_patch for q in range(n_patch)] for p in range(n_patch)]

    def mark_live(lengths, tok_rows, keep):
        rows, pitch = n_head * tok_rows, padded(keep)
        owner, within = [], []
        for p in range(n_patch):
            owner.append([p] * rows + [n_patch] * (padded(rows) - rows))
            for source in sources[p]:
                owner[p] += [source] * keep + [n_patch] * (pitch - keep)
        total = len(owner[0])
        column = lax.broadcasted_iota(jnp.int32, (1, total), 1)
        mine = lax.axis_index("head").astype(jnp.int32)
        own = lax.dynamic_slice(
            jnp.asarray(owner, jnp.int32),
            (lax.axis_index("patch").astype(jnp.uint32), jnp.uint32(0)),
            (1, total),
        )
        fresh = column ^ (mine * tok_rows)
        within = jnp.where(column < padded(rows), fresh, (column - padded(rows)) % pitch)
        patches = lax.broadcasted_iota(jnp.int32, (n_patch, total), 0)
        found = (own == patches) & (within < lengths[:, None])
        return jnp.sum(found.astype(jnp.int32), axis=0, keepdims=True)

    def shards(qkv, stale_kv, w_out, gate_table, lengths, timestep):
        keep = stale_kv.shape[0] * 3 // 4
        qkv_t = jnp.transpose(qkv, (1, 0, 2))
        stale = jnp.transpose(stale_kv[:keep], (1, 0, 2))
        stale, qkv_t = lax.optimization_barrier((stale, qkv_t))
        sent = list(split_qkv(qkv_t, n_head))
        live = mark_live(lengths, qkv.shape[0], keep)
        if on_ring:
            key_before = lax.ppermute(stale[:1], "patch", onward)
            value_before = lax.ppermute(stale[1:], "patch", onward)
            key_before, *sent[2:] = lax.optimization_barrier((key_before, *sent[2:]))
            both, _ = lax.optimization_barrier((stale, sent[0]))
            after = lax.ppermute(both, "patch", backward)
            key_two = lax.ppermute(key_before, "patch", onward)
            value_two = lax.ppermute(value_before, "patch", onward)
            keys = [(key_before, 0), (after, 0), (key_two, 0)]
            values = [(value_before, 0), (after, 1), (value_two, 0)]
        else:
            gathered = lax.all_gather(stale, "patch", axis=1, tiled=True)
            keys, values = [(gathered, 0)], [(gathered, 1)]
        pieces = [sent[0]] + [lax.ppermute(sent[j], "head", flip[j]) for j in range(1, n_head)]
        early = len(values) - 1
        weights, mixed, sums, next_t, w_held = weigh(live, pieces, keys, values[:early], w_out)
        steps = lax.broadcasted_iota(jnp.int32, gate_table.shape, 0)
        gate_row = jnp.sum(
            jnp.where(steps == timestep[:, None], gate_table.astype(jnp.float32), 0.0), axis=0, keepdims=True
        )

        def exchange(held):
            bit = 1
            while True:
                arrived = [lax.ppermute(held[j], "head", flip[bit]) for j in range(1, len(held), 2)]
                if len(arrived) == 1:
                    return held[0], arrived[0]
                held = [add_pair(held[2 * i], arrived[i]) for i in range(len(arrived))]
                bit *= 2

        half = n_head // 2
        tok_rows = qkv.shape[0]
        cut = tok_rows // HALVES
        near_cuts = [(j * tok_rows, (j + 1) * tok_rows) for j in range(half)]
        far_cuts = [
            (j * tok_rows + i * cut, j * tok_rows + (i + 1) * cut)
            for i in range(HALVES)
            for j in range(half, n_head)
        ]
        partial = project(weights, mixed, sums, values[early:], w_held, far_cuts + near_cuts)
        arrived = [
            lax.ppermute(add_pair(*exchange(partial[i * half : (i + 1) * half])), "head", flip[half])
            for i in range(HALVES)
        ]
        near = exchange(partial[HALVES * half :])
        next_t, *near = lax.optimization_barrier((next_t, *near))
        next_kv = jnp.transpose(next_t, (1, 0, 2))
        branch = finish(near, arrived, gate_row)
        return (branch, next_kv)

    return shards


def solution(mesh):
    return jax.shard_map(
        build(mesh.shape["head"], mesh.shape["patch"]),
        mesh=mesh,
        in_specs=(
            P(("groups", "patch", "head"), None, None),
            P(("groups", "patch"), None, "head"),
            P("head", None),
            P(),
            P("groups"),
            P("groups"),
        ),
        out_specs=(P(("groups", "patch", "head"), None), P(("groups", "patch"), None, "head")),
        check_vma=False,
    )
```
